512 devices in a mesh: inner: 32 (over x, y, core), outer: 16 (over z).
Axes of the slice: x: 4, y: 4, z: 16, core: 2. Of those that a mesh axis runs over, the one named last changes fastest.
Arguments:
- activations: bfloat16 [393216, 768], P(('inner', 'outer')), may hold values from -6 to 6
- out_grads: bfloat16 [393216, 768], P(('inner', 'outer')), may hold values from -0.016 to 0.016
- error_in: bfloat16 [512, 768, 768], P(('inner', 'outer')), may hold values from -4 to 4
- q_init: float32 [768, 8], replicated, may hold values from -6 to 6
Outputs:
- error_out: bfloat16 [512, 768, 768], P(('inner', 'outer'))
- p_basis: float32 [768, 8], replicated
- q_factor: float32 [768, 8], replicated
The draws below stay inside these ranges and needn't reach their ends.
All inputs are finite; a program needn't handle non-finite values.
Results may differ from the reference program's by a relative error of at most 0.0012.
Values sent between devices are 32-bit elements; how exact they have to be, the bound alone decides.
No kernel may reach another device: no remote copies, remote signals or barrier semaphores. Data moves between devices by JAX's collectives and lax.ppermute only.
A program may use at most 64 MiB of HBM per device.

```python
import math
import jax
import jax.numpy as jnp
from jax import lax

M = 768
N = 768
R = 8
TOK_DEV = 768
TOKENS = 393216
N_INNER = 32
N_OUTER = 16


def combine(coeffs, directions):
    summed = coeffs[:, 0:1] * directions[0:1, :]
    for column in range(1, directions.shape[0]):
        summed = summed + coeffs[:, column:column + 1] * directions[column:column + 1, :]
    return summed


def shared_parts(key):
    latent = jax.random.truncated_normal(jax.random.fold_in(key, 101), -4.0, 4.0, (TOKENS, R), jnp.float32)
    left_dirs = jax.random.truncated_normal(jax.random.fold_in(key, 102), -4.0, 4.0, (R, M), jnp.float32)
    right_dirs = jax.random.truncated_normal(jax.random.fold_in(key, 103), -4.0, 4.0, (R, N), jnp.float32)
    coupling = jnp.eye(R, dtype=jnp.float32) + 0.14 * jax.random.truncated_normal(jax.random.fold_in(key, 104), -4.0, 4.0, (R, R), jnp.float32)
    wobble = jax.random.truncated_normal(jax.random.fold_in(key, 105), -4.0, 4.0, (TOKENS // TOK_DEV, R, R), jnp.float32)
    return (latent, left_dirs, right_dirs, coupling, wobble)


def draw_activations(key, part):
    latent, left_dirs, right_dirs, coupling, wobble = shared_parts(key)
    key = jax.random.fold_in(key, 1)
    jitter = jax.random.truncated_normal(key, -4.0, 4.0, (TOKENS, M), jnp.float32)
    lowrank = combine(latent, left_dirs) / math.sqrt(R)
    return jnp.clip(0.8 * lowrank + 0.6 * jitter, -6.0, 6.0).astype(jnp.bfloat16)


def draw_out_grads(key, part):
    latent, left_dirs, right_dirs, coupling, wobble = shared_parts(key)
    key = jax.random.fold_in(key, 2)
    strength = 0.002
    spread = 0.76
    jitter = jax.random.truncated_normal(key, -4.0, 4.0, (TOKENS, N), jnp.float32)
    devices_all = TOKENS // TOK_DEV
    per_device = coupling[None, :, :] + spread * wobble
    blocks = latent.reshape(devices_all, TOK_DEV, R)
    mixture = blocks[:, :, 0:1] * per_device[:, 0:1, :]
    for column in range(1, R):
        mixture = mixture + blocks[:, :, column:column + 1] * per_device[:, column:column + 1, :]
    mixture = mixture.reshape(TOKENS, R) / math.sqrt(1.16 + R * spread * spread)
    lowrank = combine(mixture, right_dirs) / math.sqrt(R)
    return jnp.clip(strength * (0.8 * lowrank + 0.6 * jitter), -0.016, 0.016).astype(jnp.bfloat16)


def draw_q_init(key, part):
    latent, left_dirs, right_dirs, coupling, wobble = shared_parts(key)
    key = jax.random.fold_in(key, 3)
    jitter = jax.random.truncated_normal(key, -4.0, 4.0, (N, R), jnp.float32)
    return jnp.clip(right_dirs.T + 0.7 * jitter, -6.0, 6.0)


def levels(key, extent, cuts, least, top_value):
    loudness = 1.0
    for axis_at, shards_of in cuts:
        steps = jax.random.uniform(jax.random.fold_in(jax.random.fold_in(key, 6), axis_at), (shards_of,), jnp.float32, least / len(cuts), top_value / len(cuts))
        loudness = loudness * jnp.repeat(jnp.exp(steps), extent[axis_at] // shards_of).reshape((-1,) + (1,) * (len(extent) - 1 - axis_at))
    return loudness


def centred(rng, shape, deviation, reach, shards=(), held_as=jnp.bfloat16):
    array = jax.random.normal(rng, shape, jnp.float32) * deviation
    if len(shards) > 0:
        array = levels(rng, shape, shards, -0.22, 0.18) * array
    return jnp.clip(array, min=-reach, max=reach).astype(held_as)


def setup_inputs(seed: int = 0) -> dict:
    seeds = jax.random.split(jax.random.key(seed), 5)
    return {
        "activations": draw_activations(jax.random.fold_in(seeds[4], 71), 0),
        "out_grads": draw_out_grads(jax.random.fold_in(seeds[4], 71), 0),
        "error_in": centred(seeds[2], (N_INNER * N_OUTER, M, N), 0.25, 4.0, ((0, 512),)),
        "q_init": draw_q_init(jax.random.fold_in(seeds[4], 71), 0),
    }


precision_mode = lax.Precision.HIGHEST

def reference(activations, out_grads, error_in, q_init):
    devices_all = N_INNER * N_OUTER
    total = jnp.dot(activations.T.astype(jnp.float32), out_grads.astype(jnp.float32), preferred_element_type=jnp.float32)
    total = total + jnp.sum(error_in, axis=0, dtype=jnp.float32)
    p_sum = jnp.dot(total, q_init, precision=precision_mode)
    gram_matrix = jnp.dot(p_sum.T, p_sum, precision=precision_mode)
    lower_factor = jnp.linalg.cholesky(gram_matrix)
    p_basis = lax.linalg.triangular_solve(lower_factor, p_sum, left_side=False, lower=True, transpose_a=True)
    q_factor = jnp.dot(total.T, p_basis, precision=precision_mode)
    correction = jnp.dot(p_basis, q_factor.T, precision=precision_mode) / devices_all
    act_blocks = activations.reshape(devices_all, TOK_DEV, M)
    grad_blocks = out_grads.reshape(devices_all, TOK_DEV, N)

    def per_device(operands):
        act_rows, grad_rows, err_block = operands
        gradient = jnp.dot(act_rows.T.astype(jnp.float32), grad_rows.astype(jnp.float32), preferred_element_type=jnp.float32)
        return (gradient + err_block.astype(jnp.float32) - correction).astype(jnp.bfloat16)
    error_out = lax.map(per_device, (act_blocks, grad_blocks, error_in))
    return (error_out, p_basis, q_factor)
```

```python
import jax
import jax.numpy as jnp
from jax import lax
from jax.sharding import PartitionSpec as P

precision_mode = lax.Precision.HIGHEST


def normalize(factor, gram_matrix):
    lower_factor = jnp.linalg.cholesky(gram_matrix)
    return lax.linalg.triangular_solve(lower_factor, factor, left_side=True, lower=True)


def exchange(parts, axis, groups=None):
    return lax.all_to_all(parts, axis, 0, 0, axis_index_groups=groups)


def reduce_all(rows):
    n_inner, n_outer = lax.axis_size("inner"), lax.axis_size("outer")
    rank, width = rows.shape
    groups = [list(range(first, first + rank)) for first in range(0, n_inner, rank)]
    parts = jnp.broadcast_to(rows[None], (n_inner // rank, rank, width)).reshape(n_inner, 1, width)
    row = jnp.sum(exchange(parts, "inner"), axis=0)
    parts = jnp.broadcast_to(row[None], (n_outer, 1, width))
    row = jnp.sum(exchange(parts, "outer"), axis=0)
    parts = jnp.broadcast_to(row[None], (rank, 1, width))
    return exchange(parts, "inner", groups).reshape(rank, width)


def local(activations, out_grads, error_in, q_init):
    devices_all = lax.axis_size("inner") * lax.axis_size("outer")
    gradient = lax.dot_general(
        activations, out_grads, (((0,), (0,)), ((), ())), preferred_element_type=jnp.float32
    )
    merged = gradient + error_in[0].astype(jnp.float32)
    local_p = lax.dot_general(q_init, merged, (((0,), (1,)), ((), ())), precision=precision_mode)
    p_sum = reduce_all(local_p)
    gram_matrix = jnp.dot(p_sum, p_sum.T, precision=precision_mode)
    p_basis = normalize(p_sum, gram_matrix)
    local_q = jnp.dot(p_basis, merged, precision=precision_mode)
    q_factor = reduce_all(local_q)
    correction = lax.dot_general(
        p_basis, q_factor, (((0,), (0,)), ((), ())), precision=precision_mode
    ) / devices_all
    error_out = (merged - correction).astype(jnp.bfloat16)[None]
    return (error_out, p_basis.T, q_factor.T)


def solution(mesh):
    placed = (
        P(("inner", "outer"), None),
        P(("inner", "outer"), None),
        P(("inner", "outer"), None, None),
        P(),
    )
    return jax.shard_map(
        local,
        mesh=mesh,
        in_specs=placed,
        out_specs=(P(("inner", "outer"), None, None), P(), P()),
        check_vma=False,
    )
```

```python
import functools
import jax
import jax.numpy as jnp
from jax import lax
from jax.experimental import pallas as pl
from jax.experimental.pallas import tpu as pltpu
from jax.sharding import PartitionSpec as P

BLOCK = 256
LANES = 128
BF16 = jnp.bfloat16
F32 = jnp.float32
VMEM_BYTES = 24 * 1024 * 1024


def split(values, terms):
    found = []
    for at in range(terms):
        found.append(values.astype(BF16))
        if at + 1 < terms:
            values = values - found[-1].astype(F32)
    return found


def store_rows(parts_ref, rows, at, copies):
    rank = rows.shape[0]
    for tile in range(rows.shape[1] // LANES):
        piece = rows[:, tile * LANES:(tile + 1) * LANES]
        for copy in range(copies):
            parts_ref[copy * rank:(copy + 1) * rank, at + tile, :] = piece


def merge_kernel(a_hbm, g_hbm, e_hbm, q_hbm, hi_ref, lo_ref, parts_ref, a_buf, g_buf, e_buf, q_buf, sems):
    width, height = g_buf.shape[1], hi_ref.shape[0]
    blocks = height // BLOCK
    rank = q_buf.shape[0]
    copies = parts_ref.shape[0] // rank
    q_copy = pltpu.make_async_copy(q_hbm, q_buf, sems.at[1 + 2 * blocks])
    g_copy = pltpu.make_async_copy(g_hbm, g_buf, sems.at[0])
    a_copies, e_copies = [], []
    for b in range(blocks):
        at = pl.ds(b * BLOCK, BLOCK)
        a_copies.append(pltpu.make_async_copy(a_hbm.at[:, at], a_buf.at[b], sems.at[1 + b]))
        e_copies.append(pltpu.make_async_copy(e_hbm.at[at, :], e_buf.at[b], sems.at[1 + blocks + b]))
    a_copies[0].start()
    g_copy.start()
    q_copy.start()
    for b in range(blocks):
        if b > 0:
            a_copies[b].start()
        e_copies[b].start()
    q_copy.wait()
    q_terms = split(q_buf[...], 3)
    q_rows = jnp.concatenate(q_terms, axis=0)
    a_copies[0].wait()
    g_copy.wait()
    for b in range(blocks):
        if b > 0:
            a_copies[b].wait()
        gradient = lax.dot_general(
            a_buf[b], g_buf[...], (((0,), (0,)), ((), ())), preferred_element_type=F32
        )
        e_copies[b].wait()
        merged = gradient + e_buf[b].astype(F32)
        terms = split(merged, 3)
        at = slice(b * BLOCK, (b + 1) * BLOCK)
        hi_ref[at, :] = terms[0]
        lo_ref[at, :] = terms[1]
        total = jnp.zeros((rank, BLOCK), F32)
        for order, term in reversed(list(enumerate(terms))):
            used = (3 - order) * rank
            product = lax.dot_general(
                q_rows[:used], term, (((1,), (1,)), ((), ())), preferred_element_type=F32
            )
            for first in reversed(range(0, used, rank)):
                total = total + product[first:first + rank]
        store_rows(parts_ref, total, b * (BLOCK // LANES), copies)


def vmem(shape, dtype):
    return pltpu.VMEM(shape, dtype)


def in_vmem(x):
    return pltpu.with_memory_space_constraint(x, pltpu.VMEM)


def in_hbm(x):
    return pltpu.with_memory_space_constraint(x, pltpu.HBM)


SPEC_VMEM = pl.BlockSpec(memory_space=pltpu.VMEM)
SPEC_ANY = pl.BlockSpec(memory_space=pl.ANY)


def merge(activations, out_grads, error, q_rows, peers):
    tokens, height = activations.shape
    width = out_grads.shape[1]
    blocks = height // BLOCK
    return pl.pallas_call(
        merge_kernel,
        name="merge",
        out_shape=(
            vmem((height, width), BF16),
            vmem((height, width), BF16),
            vmem((peers, height // LANES, LANES), F32),
        ),
        in_specs=[SPEC_ANY] * 4,
        out_specs=(SPEC_VMEM,) * 3,
        scratch_shapes=[
            pltpu.VMEM((blocks, tokens, BLOCK), BF16),
            pltpu.VMEM((tokens, width), BF16),
            pltpu.VMEM((blocks, BLOCK, width), BF16),
            pltpu.VMEM(q_rows.shape, F32),
            pltpu.SemaphoreType.DMA((2 + 2 * blocks,)),
        ],
        compiler_params=pltpu.CompilerParams(vmem_limit_bytes=VMEM_BYTES),
    )(in_hbm(activations), in_hbm(out_grads), in_hbm(error), in_hbm(q_rows))


def sum_kernel(in_ref, out_ref):
    total = in_ref[0]
    for at in range(1, in_ref.shape[0]):
        total = total + in_ref[at]
    for at in range(out_ref.shape[0]):
        out_ref[at] = total


def sum_parts(parts, copies):
    return pl.pallas_call(
        sum_kernel,
        name="sum_parts",
        out_shape=vmem((copies,) + parts.shape[1:], F32),
        in_specs=[SPEC_VMEM],
        out_specs=SPEC_VMEM,
        compiler_params=pltpu.CompilerParams(vmem_limit_bytes=VMEM_BYTES),
    )(in_vmem(parts))


def load_rows(parts_ref):
    return jnp.concatenate([parts_ref[:, at, :] for at in range(parts_ref.shape[1])], axis=1)


def basis_kernel(p_ref, hi_ref, lo_ref, basis_ref, parts_ref):
    rank = p_ref.shape[0]
    copies = parts_ref.shape[0] // rank
    rows = load_rows(p_ref)
    gram = lax.dot_general(
        rows, rows, (((1,), (1,)), ((), ())),
        precision=lax.Precision.HIGHEST, preferred_element_type=F32,
    )
    index = lax.broadcasted_iota(jnp.int32, (rank, 1), 0)
    for step in range(rank):
        scale = lax.rsqrt(gram[step:step + 1, step:step + 1])
        gram_row = gram[step:step + 1, :] * scale
        row = rows[step:step + 1, :] * scale
        column = gram[:, step:step + 1] * scale
        below = index > step
        here = index == step
        gram = jnp.where(below, gram - column * gram_row, gram)
        rows = jnp.where(here, row, jnp.where(below, rows - column * row, rows))
    basis_ref[...] = rows
    terms = jnp.concatenate(split(rows, 3), axis=0)
    high = jnp.dot(terms, hi_ref[...], preferred_element_type=F32)
    low = jnp.dot(terms[:2 * rank], lo_ref[...], preferred_element_type=F32)
    total = low[rank:] + high[2 * rank:] + low[:rank] + high[rank:2 * rank] + high[:rank]
    store_rows(parts_ref, total, 0, copies)


def basis(p_parts, hi, lo, peers):
    rank, tiles, _ = p_parts.shape
    return pl.pallas_call(
        basis_kernel,
        name="basis",
        out_shape=(
            vmem((rank, tiles * LANES), F32),
            vmem((peers, hi.shape[1] // LANES, LANES), F32),
        ),
        in_specs=[SPEC_VMEM] * 3,
        out_specs=(SPEC_VMEM,) * 2,
        compiler_params=pltpu.CompilerParams(vmem_limit_bytes=VMEM_BYTES),
    )(in_vmem(p_parts), in_vmem(hi), in_vmem(lo))


def error_kernel(devices_all, q_ref, basis_ref, hi_ref, lo_ref, error_hbm, q_out_ref, basis_out_ref, buf, sems):
    blocks = buf.shape[0]
    rows = load_rows(q_ref)
    q_out_ref[...] = rows
    basis_out_ref[...] = basis_ref[...]
    b1, b2, b3 = split(basis_ref[...] / devices_all, 3)
    q1, q2, q3 = split(rows, 3)
    left = jnp.concatenate([b1, b1, b2, b1, b2, b3], axis=0)
    right = jnp.concatenate([q1, q2, q1, q3, q2, q1], axis=0)
    copies = []
    for b in range(blocks):
        at = slice(b * BLOCK, (b + 1) * BLOCK)
        correction = lax.dot_general(
            left[:, at], right, (((0,), (0,)), ((), ())), preferred_element_type=F32
        )
        merged = hi_ref[at, :].astype(F32) + lo_ref[at, :].astype(F32)
        buf[b] = (merged - correction).astype(BF16)
        copies.append(pltpu.make_async_copy(buf.at[b], error_hbm.at[0, pl.ds(b * BLOCK, BLOCK), :], sems.at[b]))
        copies[-1].start()
    for copy in copies:
        copy.wait()


def new_error(q_parts, basis_rows, hi, lo, devices_all):
    height, width = hi.shape
    rank = basis_rows.shape[0]
    blocks = height // BLOCK
    return pl.pallas_call(
        functools.partial(error_kernel, devices_all),
        name="new_error",
        out_shape=(
            jax.ShapeDtypeStruct((1, height, width), BF16),
            jax.ShapeDtypeStruct((rank, width), F32),
            jax.ShapeDtypeStruct((rank, height), F32),
        ),
        in_specs=[SPEC_VMEM] * 4,
        out_specs=(SPEC_ANY, SPEC_VMEM, SPEC_VMEM),
        scratch_shapes=[
            pltpu.VMEM((blocks, BLOCK, width), BF16),
            pltpu.SemaphoreType.DMA((blocks,)),
        ],
        compiler_params=pltpu.CompilerParams(vmem_limit_bytes=VMEM_BYTES),
    )(in_vmem(q_parts), in_vmem(basis_rows), in_vmem(hi), in_vmem(lo))


def exchange(parts, axis, groups=None):
    return lax.all_to_all(parts, axis, 0, 0, axis_index_groups=groups)


def reduce_all(parts, rank):
    n_inner, n_outer = lax.axis_size("inner"), lax.axis_size("outer")
    groups = [list(range(first, first + rank)) for first in range(0, n_inner, rank)]
    parts = sum_parts(exchange(parts, "inner"), n_outer)
    parts = sum_parts(exchange(parts, "outer"), rank)
    return exchange(parts, "inner", groups)


def local(activations, out_grads, error_in, q_init):
    n_inner, n_outer = lax.axis_size("inner"), lax.axis_size("outer")
    rank = q_init.shape[1]
    hi, lo, parts = merge(activations, out_grads, error_in[0], q_init.T, n_inner)
    basis_rows, parts = basis(reduce_all(parts, rank), hi, lo, n_inner)
    error_out, q_rows, p_rows = new_error(reduce_all(parts, rank), basis_rows, hi, lo, n_inner * n_outer)
    return (error_out, p_rows.T, q_rows.T)


def solution(mesh):
    placed = (
        P(("inner", "outer"), None),
        P(("inner", "outer"), None),
        P(("inner", "outer"), None, None),
        P(),
    )
    return jax.shard_map(
        local,
        mesh=mesh,
        in_specs=placed,
        out_specs=(P(("inner", "outer"), None, None), P(), P()),
        check_vma=False,
    )
```

```python
import functools
import jax
import jax.numpy as jnp
from jax import lax
from jax.experimental import pallas as pl
from jax.experimental.pallas import tpu as pltpu
from jax.sharding import PartitionSpec as P

BF16 = jnp.bfloat16
F32 = jnp.float32
TERMS = 3
VMEM_BYTES = 24 * 1024 * 1024
SPEC_VMEM = pl.BlockSpec(memory_space=pltpu.VMEM)
SPEC_ANY = pl.BlockSpec(memory_space=pl.ANY)
PARAMS = pltpu.CompilerParams(vmem_limit_bytes=VMEM_BYTES)


def in_hbm(x):
    return pltpu.with_memory_space_constraint(x, pltpu.HBM)


def in_vmem(x):
    return pltpu.with_memory_space_constraint(x, pltpu.VMEM)


def split(values):
    found = []
    for at in range(TERMS):
        found.append(values.astype(BF16))
        values = values - found[-1].astype(F32)
    return found


def stack(values):
    return jnp.concatenate(split(values), axis=0)


def unstack(product):
    rank = product.shape[0] // TERMS
    return product[2 * rank:] + product[rank:2 * rank] + product[:rank]


def dot_nn(left, right):
    return lax.dot_general(left, right, (((1,), (0,)), ((), ())), preferred_element_type=F32)


def dot_nt(left, right):
    return lax.dot_general(left, right, (((1,), (1,)), ((), ())), preferred_element_type=F32)


def dot_tn(left, right):
    return lax.dot_general(left, right, (((0,), (0,)), ((), ())), preferred_element_type=F32)


def store_parts(parts_ref, rows):
    for at in range(rows.shape[0]):
        parts_ref[at] = rows[at:at + 1]


def sum_rows(parts_ref, rank):
    rows = []
    for at in range(rank):
        row = parts_ref[at]
        for other in range(at + rank, parts_ref.shape[0], rank):
            row = row + parts_ref[other]
        rows.append(row)
    return jnp.concatenate(rows, axis=0)


def left_kernel(a_hbm, g_hbm, e_hbm, q_hbm, a_ref, g_ref, e_ref, parts_ref, q_buf, sems):
    pairs = ((q_hbm, q_buf), (g_hbm, g_ref), (e_hbm, e_ref), (a_hbm, a_ref))
    copies = [pltpu.make_async_copy(*pair, sems.at[at]) for at, pair in enumerate(pairs)]
    for copy in copies:
        copy.start()
    q_copy, g_copy, e_copy, a_copy = copies
    q_copy.wait()
    terms = stack(q_buf[...])
    g_copy.wait()
    tokens = stack(unstack(dot_nt(terms, g_ref[...])))
    e_copy.wait()
    from_error = unstack(dot_nt(terms, e_ref[...]))
    a_copy.wait()
    store_parts(parts_ref, unstack(dot_nn(tokens, a_ref[...])) + from_error)


def left_term(activations, out_grads, error, q_rows):
    rank, width = q_rows.shape
    height = activations.shape[1]
    return pl.pallas_call(
        left_kernel,
        name="left_term",
        out_shape=(
            pltpu.VMEM(activations.shape, BF16),
            pltpu.VMEM(out_grads.shape, BF16),
            pltpu.VMEM(error.shape, BF16),
            pltpu.VMEM((rank, 1, height), F32),
        ),
        in_specs=[SPEC_ANY] * 4,
        out_specs=(SPEC_VMEM,) * 4,
        scratch_shapes=[pltpu.VMEM(q_rows.shape, F32), pltpu.SemaphoreType.DMA((4,))],
        compiler_params=PARAMS,
    )(in_hbm(activations), in_hbm(out_grads), in_hbm(error), in_hbm(q_rows))


def sum_kernel(in_ref, out_ref):
    total = in_ref[0]
    for at in range(1, in_ref.shape[0]):
        total = total + in_ref[at]
    for at in range(out_ref.shape[0]):
        out_ref[at] = total


def sum_parts(parts, copies):
    return pl.pallas_call(
        sum_kernel,
        name="sum_parts",
        out_shape=pltpu.VMEM((copies,) + parts.shape[1:], F32),
        in_specs=[SPEC_VMEM],
        out_specs=SPEC_VMEM,
        compiler_params=PARAMS,
    )(in_vmem(parts))


def inverse_factor(rows):
    rank = rows.shape[0]
    gram = lax.dot_general(
        rows, rows, (((1,), (1,)), ((), ())),
        precision=lax.Precision.HIGHEST, preferred_element_type=F32,
    )
    index = lax.broadcasted_iota(jnp.int32, (rank, 1), 0)
    inverse = (index == lax.broadcasted_iota(jnp.int32, (rank, rank), 1)).astype(F32)
    for step in range(rank):
        at = slice(step, step + 1)
        scale = lax.rsqrt(gram[at, at])
        column = jnp.where(index > step, gram[:, at] * scale, 0.0)
        gram = gram - column * (gram[at, :] * scale)
        row = inverse[at, :] * scale
        inverse = jnp.where(index == step, row, inverse - column * row)
    return inverse


def combine(factors, rows):
    total = factors[:, 0:1] * rows[0:1, :]
    for at in range(1, rows.shape[0]):
        total = total + factors[:, at:at + 1] * rows[at:at + 1, :]
    return total


def right_kernel(p_ref, a_ref, g_ref, e_ref, basis_ref, parts_ref):
    rank = parts_ref.shape[0]
    rows = sum_rows(p_ref, rank)
    inverse = inverse_factor(rows)
    basis_ref[...] = combine(inverse, rows)
    terms = stack(rows)
    tokens = stack(unstack(dot_nt(terms, a_ref[...])))
    products = unstack(dot_nn(tokens, g_ref[...])) + unstack(dot_nn(terms, e_ref[...]))
    store_parts(parts_ref, combine(inverse, products))


def right_term(p_parts, activations, out_grads, error, rank):
    return pl.pallas_call(
        right_kernel,
        name="right_term",
        out_shape=(
            pltpu.VMEM((rank, activations.shape[1]), F32),
            pltpu.VMEM((rank, 1, out_grads.shape[1]), F32),
        ),
        in_specs=[SPEC_VMEM] * 4,
        out_specs=(SPEC_VMEM,) * 2,
        compiler_params=PARAMS,
    )(in_vmem(p_parts), in_vmem(activations), in_vmem(out_grads), in_vmem(error))


def error_kernel(devices_all, q_ref, basis_ref, a_ref, g_ref, e_ref, error_hbm, q_hbm, basis_hbm, buf, q_buf, sems):
    basis_copy = pltpu.make_async_copy(basis_ref, basis_hbm, sems.at[0])
    basis_copy.start()
    rows = sum_rows(q_ref, basis_ref.shape[0])
    q_buf[...] = rows
    q_copy = pltpu.make_async_copy(q_buf, q_hbm, sems.at[1])
    q_copy.start()
    b1, b2, b3 = split(basis_ref[...] / -devices_all)
    q1, q2, q3 = split(rows)
    left = jnp.concatenate([b1, b1, b2, b1, b2, b3], axis=0)
    right = jnp.concatenate([q1, q2, q1, q3, q2, q1], axis=0)
    merged = dot_tn(a_ref[...], g_ref[...]) + e_ref[...].astype(F32)
    buf[0] = (merged + dot_tn(left, right)).astype(BF16)
    error_copy = pltpu.make_async_copy(buf, error_hbm, sems.at[2])
    error_copy.start()
    basis_copy.wait()
    q_copy.wait()
    error_copy.wait()


def new_error(q_parts, basis_rows, activations, out_grads, error, devices_all):
    height, width = error.shape
    rank = basis_rows.shape[0]
    return pl.pallas_call(
        functools.partial(error_kernel, devices_all),
        name="new_error",
        out_shape=(
            jax.ShapeDtypeStruct((1, height, width), BF16),
            jax.ShapeDtypeStruct((rank, width), F32),
            jax.ShapeDtypeStruct((rank, height), F32),
        ),
        in_specs=[SPEC_VMEM] * 5,
        out_specs=(SPEC_ANY,) * 3,
        scratch_shapes=[
            pltpu.VMEM((1, height, width), BF16),
            pltpu.VMEM((rank, width), F32),
            pltpu.SemaphoreType.DMA((3,)),
        ],
        compiler_params=PARAMS,
    )(*[in_vmem(x) for x in (q_parts, basis_rows, activations, out_grads, error)])


def exchange(parts, axis, groups=None):
    return lax.all_to_all(parts, axis, 0, 0, axis_index_groups=groups)


def reduce_all(parts):
    rank = parts.shape[0]
    n_inner, n_outer = lax.axis_size("inner"), lax.axis_size("outer")
    groups = [list(range(first, first + rank)) for first in range(0, n_inner, rank)]
    parts = sum_parts(exchange(parts, "inner", groups), n_outer)
    parts = sum_parts(exchange(parts, "outer"), n_inner)
    return exchange(parts, "inner")


def local(activations, out_grads, error_in, q_init):
    devices_all = lax.axis_size("inner") * lax.axis_size("outer")
    *operands, parts = left_term(activations, out_grads, error_in[0], q_init.T)
    basis_rows, parts = right_term(reduce_all(parts), *operands, q_init.shape[1])
    error_out, q_rows, p_rows = new_error(reduce_all(parts), basis_rows, *operands, devices_all)
    return (error_out, p_rows.T, q_rows.T)


def solution(mesh):
    placed = (
        P(("inner", "outer"), None),
        P(("inner", "outer"), None),
        P(("inner", "outer"), None, None),
        P(),
    )
    return jax.shard_map(
        local,
        mesh=mesh,
        in_specs=placed,
        out_specs=(P(("inner", "outer"), None, None), P(), P()),
        check_vma=False,
    )
```

```python
import functools
import jax
import jax.numpy as jnp
from jax import lax
from jax.experimental import pallas as pl
from jax.experimental.pallas import tpu as pltpu
from jax.sharding import PartitionSpec as P

BF16 = jnp.bfloat16
F32 = jnp.float32
TERMS = 3
VMEM_BYTES = 24 * 1024 * 1024
SPEC_VMEM = pl.BlockSpec(memory_space=pltpu.VMEM)
SPEC_ANY = pl.BlockSpec(memory_space=pl.ANY)
PARAMS = pltpu.CompilerParams(vmem_limit_bytes=VMEM_BYTES)


def in_hbm(x):
    return pltpu.with_memory_space_constraint(x, pltpu.HBM)


def in_vmem(x):
    return pltpu.with_memory_space_constraint(x, pltpu.VMEM)


def split(values):
    found = []
    for at in range(TERMS):
        found.append(values.astype(BF16))
        values = values - found[-1].astype(F32)
    return found


def stack(values):
    return jnp.concatenate(split(values), axis=0)


def unstack(product):
    rank = product.shape[0] // TERMS
    return product[2 * rank:] + product[rank:2 * rank] + product[:rank]


def dot_nn(left, right):
    return lax.dot_general(left, right, (((1,), (0,)), ((), ())), preferred_element_type=F32)


def dot_nt(left, right):
    return lax.dot_general(left, right, (((1,), (1,)), ((), ())), preferred_element_type=F32)


def dot_tn(left, right):
    return lax.dot_general(left, right, (((0,), (0,)), ((), ())), preferred_element_type=F32)


def store_parts(parts_ref, rows):
    for at in range(rows.shape[0]):
        parts_ref[at] = rows[at:at + 1]


def sum_rows(parts_ref, rank):
    rows = []
    for at in range(rank):
        row = parts_ref[at]
        for other in range(at + rank, parts_ref.shape[0], rank):
            row = row + parts_ref[other]
        rows.append(row)
    return jnp.concatenate(rows, axis=0)


def has_time(n_outer):
    at = lax.axis_index("outer")
    return (at <= n_outer // 4) | (at >= n_outer - n_outer // 4)


def left_kernel(n_outer, a_hbm, g_hbm, e_hbm, q_hbm, a_ref, g_ref, e_ref, merged_ref, parts_ref, q_buf, sems):
    pairs = ((q_hbm, q_buf), (g_hbm, g_ref), (e_hbm, e_ref), (a_hbm, a_ref))
    copies = [pltpu.make_async_copy(*pair, sems.at[at]) for at, pair in enumerate(pairs)]
    for copy in copies:
        copy.start()
    q_copy, g_copy, e_copy, a_copy = copies
    q_copy.wait()
    terms = stack(q_buf[...])
    g_copy.wait()
    tokens = stack(unstack(dot_nt(terms, g_ref[...])))
    e_copy.wait()
    from_error = unstack(dot_nt(terms, e_ref[...]))
    a_copy.wait()
    store_parts(parts_ref, unstack(dot_nn(tokens, a_ref[...])) + from_error)

    @pl.when(has_time(n_outer))
    def _():
        merged_ref[...] = dot_tn(a_ref[...], g_ref[...]) + e_ref[...].astype(F32)


def left_term(activations, out_grads, error, q_rows, n_outer):
    rank, width = q_rows.shape
    height = activations.shape[1]
    return pl.pallas_call(
        functools.partial(left_kernel, n_outer),
        name="left_term",
        out_shape=(
            pltpu.VMEM(activations.shape, BF16),
            pltpu.VMEM(out_grads.shape, BF16),
            pltpu.VMEM(error.shape, BF16),
            pltpu.VMEM(error.shape, F32),
            pltpu.VMEM((rank, 1, height), F32),
        ),
        in_specs=[SPEC_ANY] * 4,
        out_specs=(SPEC_VMEM,) * 5,
        scratch_shapes=[pltpu.VMEM(q_rows.shape, F32), pltpu.SemaphoreType.DMA((4,))],
        compiler_params=PARAMS,
    )(in_hbm(activations), in_hbm(out_grads), in_hbm(error), in_hbm(q_rows))


def sum_kernel(in_ref, out_ref):
    total = in_ref[0]
    for at in range(1, in_ref.shape[0]):
        total = total + in_ref[at]
    for at in range(out_ref.shape[0]):
        out_ref[at] = total


def sum_parts(parts, copies):
    return pl.pallas_call(
        sum_kernel,
        name="sum_parts",
        out_shape=pltpu.VMEM((copies,) + parts.shape[1:], F32),
        in_specs=[SPEC_VMEM],
        out_specs=SPEC_VMEM,
        compiler_params=PARAMS,
    )(in_vmem(parts))


def inverse_factor(rows):
    rank = rows.shape[0]
    gram = lax.dot_general(
        rows, rows, (((1,), (1,)), ((), ())),
        precision=lax.Precision.HIGHEST, preferred_element_type=F32,
    )
    index = lax.broadcasted_iota(jnp.int32, (rank, 1), 0)
    inverse = (index == lax.broadcasted_iota(jnp.int32, (rank, rank), 1)).astype(F32)
    for step in range(rank):
        at = slice(step, step + 1)
        scale = lax.rsqrt(gram[at, at])
        column = jnp.where(index > step, gram[:, at] * scale, 0.0)
        gram = gram - column * (gram[at, :] * scale)
        row = inverse[at, :] * scale
        inverse = jnp.where(index == step, row, inverse - column * row)
    return inverse


def combine(factors, rows):
    total = factors[:, 0:1] * rows[0:1, :]
    for at in range(1, rows.shape[0]):
        total = total + factors[:, at:at + 1] * rows[at:at + 1, :]
    return total


def right_kernel(p_ref, a_ref, g_ref, e_ref, basis_ref, parts_ref):
    rank = parts_ref.shape[0]
    rows = sum_rows(p_ref, rank)
    inverse = inverse_factor(rows)
    basis_ref[...] = combine(inverse, rows)
    terms = stack(rows)
    tokens = stack(unstack(dot_nt(terms, a_ref[...])))
    products = unstack(dot_nn(tokens, g_ref[...])) + unstack(dot_nn(terms, e_ref[...]))
    store_parts(parts_ref, combine(inverse, products))


def right_term(p_parts, activations, out_grads, error, rank):
    return pl.pallas_call(
        right_kernel,
        name="right_term",
        out_shape=(
            pltpu.VMEM((rank, activations.shape[1]), F32),
            pltpu.VMEM((rank, 1, out_grads.shape[1]), F32),
        ),
        in_specs=[SPEC_VMEM] * 4,
        out_specs=(SPEC_VMEM,) * 2,
        compiler_params=PARAMS,
    )(in_vmem(p_parts), in_vmem(activations), in_vmem(out_grads), in_vmem(error))


def error_kernel(
    n_outer, devices_all, q_ref, basis_ref, a_ref, g_ref, e_ref, merged_ref,
    error_hbm, q_hbm, basis_hbm, buf, q_buf, sems,
):
    basis_copy = pltpu.make_async_copy(basis_ref, basis_hbm, sems.at[0])
    basis_copy.start()
    rows = sum_rows(q_ref, basis_ref.shape[0])
    q_buf[...] = rows
    q_copy = pltpu.make_async_copy(q_buf, q_hbm, sems.at[1])
    q_copy.start()
    b1, b2, b3 = split(basis_ref[...] / -devices_all)
    q1, q2, q3 = split(rows)
    left = jnp.concatenate([b1, b1, b2, b1, b2, b3], axis=0)
    right = jnp.concatenate([q1, q2, q1, q3, q2, q1], axis=0)
    early = has_time(n_outer)

    @pl.when(early)
    def _():
        buf[0] = (merged_ref[...] + dot_tn(left, right)).astype(BF16)

    @pl.when(jnp.logical_not(early))
    def _():
        merged = dot_tn(a_ref[...], g_ref[...]) + e_ref[...].astype(F32)
        buf[0] = (merged + dot_tn(left, right)).astype(BF16)

    error_copy = pltpu.make_async_copy(buf, error_hbm, sems.at[2])
    error_copy.start()
    basis_copy.wait()
    q_copy.wait()
    error_copy.wait()


def new_error(q_parts, basis_rows, activations, out_grads, error, merged, n_outer, devices_all):
    height, width = error.shape
    rank = basis_rows.shape[0]
    return pl.pallas_call(
        functools.partial(error_kernel, n_outer, devices_all),
        name="new_error",
        out_shape=(
            jax.ShapeDtypeStruct((1, height, width), BF16),
            jax.ShapeDtypeStruct((rank, width), F32),
            jax.ShapeDtypeStruct((rank, height), F32),
        ),
        in_specs=[SPEC_VMEM] * 6,
        out_specs=(SPEC_ANY,) * 3,
        scratch_shapes=[
            pltpu.VMEM((1, height, width), BF16),
            pltpu.VMEM((rank, width), F32),
            pltpu.SemaphoreType.DMA((3,)),
        ],
        compiler_params=PARAMS,
    )(*[in_vmem(x) for x in (q_parts, basis_rows, activations, out_grads, error, merged)])


def exchange(parts, axis, groups=None):
    return lax.all_to_all(parts, axis, 0, 0, axis_index_groups=groups)


def reduce_all(parts):
    rank = parts.shape[0]
    n_inner, n_outer = lax.axis_size("inner"), lax.axis_size("outer")
    groups = [list(range(first, first + rank)) for first in range(0, n_inner, rank)]
    parts = sum_parts(exchange(parts, "inner", groups), n_outer)
    parts = sum_parts(exchange(parts, "outer"), n_inner)
    return exchange(parts, "inner")


def local(activations, out_grads, error_in, q_init):
    n_outer = lax.axis_size("outer")
    devices_all = lax.axis_size("inner") * n_outer
    *operands, merged, parts = left_term(activations, out_grads, error_in[0], q_init.T, n_outer)
    basis_rows, parts = right_term(reduce_all(parts), *operands, q_init.shape[1])
    error_out, q_rows, p_rows = new_error(reduce_all(parts), basis_rows, *operands, merged, n_outer, devices_all)
    return (error_out, p_rows.T, q_rows.T)


def solution(mesh):
    placed = (
        P(("inner", "outer"), None),
        P(("inner", "outer"), None),
        P(("inner", "outer"), None, None),
        P(),
    )
    return jax.shard_map(
        local,
        mesh=mesh,
        in_specs=placed,
        out_specs=(P(("inner", "outer"), None, None), P(), P()),
        check_vma=False,
    )
```

```python
import functools
import jax
import jax.numpy as jnp
from jax import lax
from jax.experimental import pallas as pl
from jax.experimental.pallas import tpu as pltpu
from jax.sharding import PartitionSpec as P

BLOCK = 256
BF16 = jnp.bfloat16
F32 = jnp.float32
TERMS = 3
VMEM_BYTES = 24 * 1024 * 1024
SPEC_VMEM = pl.BlockSpec(memory_space=pltpu.VMEM)
SPEC_ANY = pl.BlockSpec(memory_space=pl.ANY)
PARAMS = pltpu.CompilerParams(vmem_limit_bytes=VMEM_BYTES)


def in_hbm(x):
    return pltpu.with_memory_space_constraint(x, pltpu.HBM)


def in_vmem(x):
    return pltpu.with_memory_space_constraint(x, pltpu.VMEM)


def split(values):
    found = []
    for at in range(TERMS):
        found.append(values.astype(BF16))
        values = values - found[-1].astype(F32)
    return found


def stack(values):
    return jnp.concatenate(split(values), axis=0)


def unstack(product):
    rank = product.shape[0] // TERMS
    return product[2 * rank:] + product[rank:2 * rank] + product[:rank]


def dot_nn(left, right):
    return lax.dot_general(left, right, (((1,), (0,)), ((), ())), preferred_element_type=F32)


def dot_nt(left, right):
    return lax.dot_general(left, right, (((1,), (1,)), ((), ())), preferred_element_type=F32)


def dot_tn(left, right):
    return lax.dot_general(left, right, (((0,), (0,)), ((), ())), preferred_element_type=F32)


def store_parts(parts_ref, rows):
    for at in range(rows.shape[0]):
        parts_ref[at] = rows[at:at + 1]


def sum_rows(parts_ref, rank):
    rows = []
    for at in range(rank):
        row = parts_ref[at]
        for other in range(at + rank, parts_ref.shape[0], rank):
            row = row + parts_ref[other]
        rows.append(row)
    return jnp.concatenate(rows, axis=0)


def has_time(n_outer):
    at = lax.axis_index("outer")
    return (at <= n_outer // 4) | (at >= n_outer - n_outer // 4)


def left_kernel(n_outer, a_hbm, g_hbm, e_hbm, q_hbm, a_ref, g_ref, e_ref, merged_ref, parts_ref, q_buf, sems):
    pairs = ((q_hbm, q_buf), (g_hbm, g_ref), (e_hbm, e_ref), (a_hbm, a_ref))
    copies = [pltpu.make_async_copy(*pair, sems.at[at]) for at, pair in enumerate(pairs)]
    for copy in copies:
        copy.start()
    q_copy, g_copy, e_copy, a_copy = copies
    q_copy.wait()
    terms = stack(q_buf[...])
    g_copy.wait()
    tokens = stack(unstack(dot_nt(terms, g_ref[...])))
    e_copy.wait()
    from_error = unstack(dot_nt(terms, e_ref[...]))
    a_copy.wait()
    store_parts(parts_ref, unstack(dot_nn(tokens, a_ref[...])) + from_error)

    @pl.when(has_time(n_outer))
    def _():
        merged_ref[...] = dot_tn(a_ref[...], g_ref[...]) + e_ref[...].astype(F32)


def left_term(activations, out_grads, error, q_rows, n_outer):
    rank, width = q_rows.shape
    height = activations.shape[1]
    return pl.pallas_call(
        functools.partial(left_kernel, n_outer),
        name="left_term",
        out_shape=(
            pltpu.VMEM(activations.shape, BF16),
            pltpu.VMEM(out_grads.shape, BF16),
            pltpu.VMEM(error.shape, BF16),
            pltpu.VMEM(error.shape, F32),
            pltpu.VMEM((rank, 1, height), F32),
        ),
        in_specs=[SPEC_ANY] * 4,
        out_specs=(SPEC_VMEM,) * 5,
        scratch_shapes=[pltpu.VMEM(q_rows.shape, F32), pltpu.SemaphoreType.DMA((4,))],
        compiler_params=PARAMS,
    )(in_hbm(activations), in_hbm(out_grads), in_hbm(error), in_hbm(q_rows))


def sum_kernel(in_ref, out_ref):
    total = in_ref[0]
    for at in range(1, in_ref.shape[0]):
        total = total + in_ref[at]
    for at in range(out_ref.shape[0]):
        out_ref[at] = total


def sum_parts(parts, copies):
    return pl.pallas_call(
        sum_kernel,
        name="sum_parts",
        out_shape=pltpu.VMEM((copies,) + parts.shape[1:], F32),
        in_specs=[SPEC_VMEM],
        out_specs=SPEC_VMEM,
        compiler_params=PARAMS,
    )(in_vmem(parts))


def inverse_factor(rows):
    rank = rows.shape[0]
    gram = lax.dot_general(
        rows, rows, (((1,), (1,)), ((), ())),
        precision=lax.Precision.HIGHEST, preferred_element_type=F32,
    )
    index = lax.broadcasted_iota(jnp.int32, (rank, 1), 0)
    inverse = (index == lax.broadcasted_iota(jnp.int32, (rank, rank), 1)).astype(F32)
    for step in range(rank):
        at = slice(step, step + 1)
        scale = lax.rsqrt(gram[at, at])
        column = jnp.where(index > step, gram[:, at] * scale, 0.0)
        gram = gram - column * (gram[at, :] * scale)
        row = inverse[at, :] * scale
        inverse = jnp.where(index == step, row, inverse - column * row)
    return inverse


def combine(factors, rows):
    total = factors[:, 0:1] * rows[0:1, :]
    for at in range(1, rows.shape[0]):
        total = total + factors[:, at:at + 1] * rows[at:at + 1, :]
    return total


def right_kernel(p_ref, a_ref, g_ref, e_ref, basis_ref, parts_ref):
    rank = parts_ref.shape[0]
    rows = sum_rows(p_ref, rank)
    inverse = inverse_factor(rows)
    basis_ref[...] = combine(inverse, rows)
    terms = stack(rows)
    tokens = stack(unstack(dot_nt(terms, a_ref[...])))
    products = unstack(dot_nn(tokens, g_ref[...])) + unstack(dot_nn(terms, e_ref[...]))
    store_parts(parts_ref, combine(inverse, products))


def right_term(p_parts, activations, out_grads, error, rank):
    return pl.pallas_call(
        right_kernel,
        name="right_term",
        out_shape=(
            pltpu.VMEM((rank, activations.shape[1]), F32),
            pltpu.VMEM((rank, 1, out_grads.shape[1]), F32),
        ),
        in_specs=[SPEC_VMEM] * 4,
        out_specs=(SPEC_VMEM,) * 2,
        compiler_params=PARAMS,
    )(in_vmem(p_parts), in_vmem(activations), in_vmem(out_grads), in_vmem(error))


def error_kernel(
    n_outer, devices_all, q_ref, basis_ref, a_ref, g_ref, e_ref, merged_ref,
    error_hbm, q_hbm, basis_hbm, buf, q_buf, sems,
):
    basis_copy = pltpu.make_async_copy(basis_ref, basis_hbm, sems.at[0])
    basis_copy.start()
    rows = sum_rows(q_ref, basis_ref.shape[0])
    q_buf[...] = rows
    q_copy = pltpu.make_async_copy(q_buf, q_hbm, sems.at[1])
    q_copy.start()
    b1, b2, b3 = split(basis_ref[...] / -devices_all)
    q1, q2, q3 = split(rows)
    left = jnp.concatenate([b1, b1, b2, b1, b2, b3], axis=0)
    right = jnp.concatenate([q1, q2, q1, q3, q2, q1], axis=0)
    early = has_time(n_outer)

    @pl.when(early)
    def _():
        height = buf.shape[1]
        copies = []
        for first in range(0, height, BLOCK):
            at = slice(first, first + BLOCK)
            buf[0, at, :] = (merged_ref[at, :] + dot_tn(left[:, at], right)).astype(BF16)
            rows_at = pl.ds(first, BLOCK)
            copies.append(pltpu.make_async_copy(
                buf.at[:, rows_at], error_hbm.at[:, rows_at], sems.at[2 + first // BLOCK]
            ))
            copies[-1].start()
        for copy in copies:
            copy.wait()

    @pl.when(jnp.logical_not(early))
    def _():
        merged = dot_tn(a_ref[...], g_ref[...]) + e_ref[...].astype(F32)
        buf[0] = (merged + dot_tn(left, right)).astype(BF16)
        copy = pltpu.make_async_copy(buf, error_hbm, sems.at[2])
        copy.start()
        copy.wait()

    basis_copy.wait()
    q_copy.wait()


def new_error(q_parts, basis_rows, activations, out_grads, error, merged, n_outer, devices_all):
    height, width = error.shape
    rank = basis_rows.shape[0]
    return pl.pallas_call(
        functools.partial(error_kernel, n_outer, devices_all),
        name="new_error",
        out_shape=(
            jax.ShapeDtypeStruct((1, height, width), BF16),
            jax.ShapeDtypeStruct((rank, width), F32),
            jax.ShapeDtypeStruct((rank, height), F32),
        ),
        in_specs=[SPEC_VMEM] * 6,
        out_specs=(SPEC_ANY,) * 3,
        scratch_shapes=[
            pltpu.VMEM((1, height, width), BF16),
            pltpu.VMEM((rank, width), F32),
            pltpu.SemaphoreType.DMA((2 + height // BLOCK,)),
        ],
        compiler_params=PARAMS,
    )(*[in_vmem(x) for x in (q_parts, basis_rows, activations, out_grads, error, merged)])


def exchange(parts, axis, groups=None):
    return lax.all_to_all(parts, axis, 0, 0, axis_index_groups=groups)


def reduce_all(parts):
    rank = parts.shape[0]
    n_inner, n_outer = lax.axis_size("inner"), lax.axis_size("outer")
    groups = [list(range(first, first + rank)) for first in range(0, n_inner, rank)]
    parts = sum_parts(exchange(parts, "inner", groups), n_outer)
    parts = sum_parts(exchange(parts, "outer"), n_inner)
    return exchange(parts, "inner")


def local(activations, out_grads, error_in, q_init):
    n_outer = lax.axis_size("outer")
    devices_all = lax.axis_size("inner") * n_outer
    *operands, merged, parts = left_term(activations, out_grads, error_in[0], q_init.T, n_outer)
    basis_rows, parts = right_term(reduce_all(parts), *operands, q_init.shape[1])
    error_out, q_rows, p_rows = new_error(reduce_all(parts), basis_rows, *operands, merged, n_outer, devices_all)
    return (error_out, p_rows.T, q_rows.T)


def solution(mesh):
    placed = (
        P(("inner", "outer"), None),
        P(("inner", "outer"), None),
        P(("inner", "outer"), None, None),
        P(),
    )
    return jax.shard_map(
        local,
        mesh=mesh,
        in_specs=placed,
        out_specs=(P(("inner", "outer"), None, None), P(), P()),
        check_vma=False,
    )
```

```python
import functools
import jax
import jax.numpy as jnp
from jax import lax
from jax.experimental import pallas as pl
from jax.experimental.pallas import tpu as pltpu
from jax.sharding import PartitionSpec as P

BLOCK = 256
PAIR = 2
FIRST = ((1, 2), (3, 0))
LAST = ((0, 1), (2, 3))
BF16 = jnp.bfloat16
F32 = jnp.float32
TERMS = 3
VMEM_BYTES = 24 * 1024 * 1024
SPEC_VMEM = pl.BlockSpec(memory_space=pltpu.VMEM)
SPEC_ANY = pl.BlockSpec(memory_space=pl.ANY)
PARAMS = pltpu.CompilerParams(vmem_limit_bytes=VMEM_BYTES)


def in_hbm(x):
    return pltpu.with_memory_space_constraint(x, pltpu.HBM)


def in_vmem(x):
    return pltpu.with_memory_space_constraint(x, pltpu.VMEM)


def split(values):
    found = []
    for at in range(TERMS):
        found.append(values.astype(BF16))
        values = values - found[-1].astype(F32)
    return found


def stack(values):
    return jnp.concatenate(split(values), axis=0)


def unstack(product):
    rank = product.shape[0] // TERMS
    return product[2 * rank:] + product[rank:2 * rank] + product[:rank]


def dot_nn(left, right):
    return lax.dot_general(left, right, (((1,), (0,)), ((), ())), preferred_element_type=F32)


def dot_nt(left, right):
    return lax.dot_general(left, right, (((1,), (1,)), ((), ())), preferred_element_type=F32)


def dot_tn(left, right):
    return lax.dot_general(left, right, (((0,), (0,)), ((), ())), preferred_element_type=F32)


def store_parts(parts_ref, rows):
    copies = parts_ref.shape[0] // rows.shape[0]
    for at in range(parts_ref.shape[0]):
        parts_ref[at] = rows[at // copies:at // copies + 1]


def sum_rows(parts_ref, rank):
    rows = []
    for at in range(rank):
        row = parts_ref[at]
        for other in range(at + rank, parts_ref.shape[0], rank):
            row = row + parts_ref[other]
        rows.append(row)
    return jnp.concatenate(rows, axis=0)


def has_time(n_outer):
    at = lax.axis_index("outer")
    return (at <= n_outer // 4) | (at >= n_outer - n_outer // 4)


def left_kernel(n_outer, a_hbm, g_hbm, e_hbm, q_hbm, a_ref, g_ref, e_ref, merged_ref, parts_ref, q_buf, sems):
    pairs = ((q_hbm, q_buf), (g_hbm, g_ref), (e_hbm, e_ref), (a_hbm, a_ref))
    copies = [pltpu.make_async_copy(*pair, sems.at[at]) for at, pair in enumerate(pairs)]
    for copy in copies:
        copy.start()
    q_copy, g_copy, e_copy, a_copy = copies
    q_copy.wait()
    terms = stack(q_buf[...])
    g_copy.wait()
    tokens = stack(unstack(dot_nt(terms, g_ref[...])))
    e_copy.wait()
    from_error = unstack(dot_nt(terms, e_ref[...]))
    a_copy.wait()
    store_parts(parts_ref, unstack(dot_nn(tokens, a_ref[...])) + from_error)

    @pl.when(has_time(n_outer))
    def _():
        merged_ref[...] = dot_tn(a_ref[...], g_ref[...]) + e_ref[...].astype(F32)


def left_term(activations, out_grads, error, q_rows, n_outer):
    rank, width = q_rows.shape
    height = activations.shape[1]
    return pl.pallas_call(
        functools.partial(left_kernel, n_outer),
        name="left_term",
        out_shape=(
            pltpu.VMEM(activations.shape, BF16),
            pltpu.VMEM(out_grads.shape, BF16),
            pltpu.VMEM(error.shape, BF16),
            pltpu.VMEM(error.shape, F32),
            pltpu.VMEM((PAIR * rank, 1, height), F32),
        ),
        in_specs=[SPEC_ANY] * 4,
        out_specs=(SPEC_VMEM,) * 5,
        scratch_shapes=[pltpu.VMEM(q_rows.shape, F32), pltpu.SemaphoreType.DMA((4,))],
        compiler_params=PARAMS,
    )(in_hbm(activations), in_hbm(out_grads), in_hbm(error), in_hbm(q_rows))


def sum_kernel(in_ref, out_ref):
    total = in_ref[0]
    for at in range(1, in_ref.shape[0]):
        total = total + in_ref[at]
    for at in range(out_ref.shape[0]):
        out_ref[at] = total


def sum_parts(parts, copies):
    return pl.pallas_call(
        sum_kernel,
        name="sum_parts",
        out_shape=pltpu.VMEM((copies,) + parts.shape[1:], F32),
        in_specs=[SPEC_VMEM],
        out_specs=SPEC_VMEM,
        compiler_params=PARAMS,
    )(in_vmem(parts))


def inverse_factor(rows):
    rank = rows.shape[0]
    gram = lax.dot_general(
        rows, rows, (((1,), (1,)), ((), ())),
        precision=lax.Precision.HIGHEST, preferred_element_type=F32,
    )
    index = lax.broadcasted_iota(jnp.int32, (rank, 1), 0)
    inverse = (index == lax.broadcasted_iota(jnp.int32, (rank, rank), 1)).astype(F32)
    for step in range(rank):
        at = slice(step, step + 1)
        scale = lax.rsqrt(gram[at, at])
        column = jnp.where(index > step, gram[:, at] * scale, 0.0)
        gram = gram - column * (gram[at, :] * scale)
        row = inverse[at, :] * scale
        inverse = jnp.where(index == step, row, inverse - column * row)
    return inverse


def combine(factors, rows):
    total = factors[:, 0:1] * rows[0:1, :]
    for at in range(1, rows.shape[0]):
        total = total + factors[:, at:at + 1] * rows[at:at + 1, :]
    return total


def right_kernel(p_ref, a_ref, g_ref, e_ref, basis_ref, parts_ref):
    rank = basis_ref.shape[0]
    rows = sum_rows(p_ref, rank)
    inverse = inverse_factor(rows)
    basis_ref[...] = combine(inverse, rows)
    terms = stack(rows)
    tokens = stack(unstack(dot_nt(terms, a_ref[...])))
    products = unstack(dot_nn(tokens, g_ref[...])) + unstack(dot_nn(terms, e_ref[...]))
    store_parts(parts_ref, combine(inverse, products))


def right_term(p_parts, activations, out_grads, error, rank):
    return pl.pallas_call(
        right_kernel,
        name="right_term",
        out_shape=(
            pltpu.VMEM((rank, activations.shape[1]), F32),
            pltpu.VMEM((PAIR * rank, 1, out_grads.shape[1]), F32),
        ),
        in_specs=[SPEC_VMEM] * 4,
        out_specs=(SPEC_VMEM,) * 2,
        compiler_params=PARAMS,
    )(in_vmem(p_parts), in_vmem(activations), in_vmem(out_grads), in_vmem(error))


def error_kernel(
    n_outer, devices_all, q_ref, basis_ref, a_ref, g_ref, e_ref, merged_ref,
    error_hbm, q_hbm, basis_hbm, buf, q_buf, sems,
):
    basis_copy = pltpu.make_async_copy(basis_ref, basis_hbm, sems.at[0])
    basis_copy.start()
    rows = sum_rows(q_ref, basis_ref.shape[0])
    q_buf[...] = rows
    q_copy = pltpu.make_async_copy(q_buf, q_hbm, sems.at[1])
    q_copy.start()
    b1, b2, b3 = split(basis_ref[...] / -devices_all)
    q1, q2, q3 = split(rows)
    left = jnp.concatenate([b1, b1, b2, b1, b2, b3], axis=0)
    right = jnp.concatenate([q1, q2, q1, q3, q2, q1], axis=0)
    early = has_time(n_outer)

    @pl.when(early)
    def _():
        height = buf.shape[1]
        copies = []
        for first in range(0, height, BLOCK):
            at = slice(first, first + BLOCK)
            buf[0, at, :] = (merged_ref[at, :] + dot_tn(left[:, at], right)).astype(BF16)
            rows_at = pl.ds(first, BLOCK)
            copies.append(pltpu.make_async_copy(
                buf.at[:, rows_at], error_hbm.at[:, rows_at], sems.at[2 + first // BLOCK]
            ))
            copies[-1].start()
        for copy in copies:
            copy.wait()

    @pl.when(jnp.logical_not(early))
    def _():
        merged = dot_tn(a_ref[...], g_ref[...]) + e_ref[...].astype(F32)
        buf[0] = (merged + dot_tn(left, right)).astype(BF16)
        copy = pltpu.make_async_copy(buf, error_hbm, sems.at[2])
        copy.start()
        copy.wait()

    basis_copy.wait()
    q_copy.wait()


def new_error(q_parts, basis_rows, activations, out_grads, error, merged, n_outer, devices_all):
    height, width = error.shape
    rank = basis_rows.shape[0]
    return pl.pallas_call(
        functools.partial(error_kernel, n_outer, devices_all),
        name="new_error",
        out_shape=(
            jax.ShapeDtypeStruct((1, height, width), BF16),
            jax.ShapeDtypeStruct((rank, width), F32),
            jax.ShapeDtypeStruct((rank, height), F32),
        ),
        in_specs=[SPEC_VMEM] * 6,
        out_specs=(SPEC_ANY,) * 3,
        scratch_shapes=[
            pltpu.VMEM((1, height, width), BF16),
            pltpu.VMEM((rank, width), F32),
            pltpu.SemaphoreType.DMA((2 + height // BLOCK,)),
        ],
        compiler_params=PARAMS,
    )(*[in_vmem(x) for x in (q_parts, basis_rows, activations, out_grads, error, merged)])


def exchange(parts, axis, groups=None):
    return lax.all_to_all(parts, axis, 0, 0, axis_index_groups=groups)


def reduce_all(parts):
    rank = parts.shape[0] // PAIR
    n_outer = lax.axis_size("outer")
    within = [[x * rank + k for k in range(rank) for x in pair] for pair in FIRST]
    across = [[x * rank + k for x in pair for k in range(rank)] for pair in LAST]
    parts = sum_parts(exchange(parts, "inner", within), n_outer)
    parts = sum_parts(exchange(parts, "outer"), PAIR * rank)
    return exchange(parts, "inner", across)


def local(activations, out_grads, error_in, q_init):
    n_outer = lax.axis_size("outer")
    devices_all = lax.axis_size("inner") * n_outer
    *operands, merged, parts = left_term(activations, out_grads, error_in[0], q_init.T, n_outer)
    basis_rows, parts = right_term(reduce_all(parts), *operands, q_init.shape[1])
    error_out, q_rows, p_rows = new_error(reduce_all(parts), basis_rows, *operands, merged, n_outer, devices_all)
    return (error_out, p_rows.T, q_rows.T)


def solution(mesh):
    placed = (
        P(("inner", "outer"), None),
        P(("inner", "outer"), None),
        P(("inner", "outer"), None, None),
        P(),
    )
    return jax.shard_map(
        local,
        mesh=mesh,
        in_specs=placed,
        out_specs=(P(("inner", "outer"), None, None), P(), P()),
        check_vma=False,
    )
```

```python
import functools
import jax
import jax.numpy as jnp
from jax import lax
from jax.experimental import pallas as pl
from jax.experimental.pallas import tpu as pltpu
from jax.sharding import PartitionSpec as P

BLOCK = 256
PAIR = 2
FIRST = ((1, 2), (3, 0))
LAST = ((0, 1), (2, 3))
BF16 = jnp.bfloat16
F32 = jnp.float32
TERMS = 3
VMEM_BYTES = 24 * 1024 * 1024
SPEC_VMEM = pl.BlockSpec(memory_space=pltpu.VMEM)
SPEC_ANY = pl.BlockSpec(memory_space=pl.ANY)
PARAMS = pltpu.CompilerParams(vmem_limit_bytes=VMEM_BYTES)


def in_hbm(x):
    return pltpu.with_memory_space_constraint(x, pltpu.HBM)


def in_vmem(x):
    return pltpu.with_memory_space_constraint(x, pltpu.VMEM)


def split(values):
    found = []
    for at in range(TERMS):
        found.append(values.astype(BF16))
        values = values - found[-1].astype(F32)
    return found


def stack(values):
    return jnp.concatenate(split(values), axis=0)


def unstack(product):
    rank = product.shape[0] // TERMS
    return product[2 * rank:] + product[rank:2 * rank] + product[:rank]


def dot_nn(left, right):
    return lax.dot_general(left, right, (((1,), (0,)), ((), ())), preferred_element_type=F32)


def dot_nt(left, right):
    return lax.dot_general(left, right, (((1,), (1,)), ((), ())), preferred_element_type=F32)


def dot_tn(left, right):
    return lax.dot_general(left, right, (((0,), (0,)), ((), ())), preferred_element_type=F32)


def store_parts(parts_ref, rows):
    copies = parts_ref.shape[0] // rows.shape[0]
    for at in range(parts_ref.shape[0]):
        parts_ref[at] = rows[at // copies:at // copies + 1]


def sum_rows(parts_ref, rank):
    rows = []
    for at in range(rank):
        row = parts_ref[at]
        for other in range(at + rank, parts_ref.shape[0], rank):
            row = row + parts_ref[other]
        rows.append(row)
    return jnp.concatenate(rows, axis=0)


def has_time(n_outer):
    at = lax.axis_index("outer")
    return (at <= n_outer // 4) | (at >= n_outer - n_outer // 4)


def left_kernel(n_outer, a_hbm, g_hbm, e_hbm, q_hbm, a_ref, g_ref, e_ref, merged_ref, parts_ref, q_buf, sems):
    pairs = ((q_hbm, q_buf), (g_hbm, g_ref), (e_hbm, e_ref), (a_hbm, a_ref))
    copies = [pltpu.make_async_copy(*pair, sems.at[at]) for at, pair in enumerate(pairs)]
    for copy in copies:
        copy.start()
    q_copy, g_copy, e_copy, a_copy = copies
    q_copy.wait()
    terms = stack(q_buf[...])
    g_copy.wait()
    tokens = stack(unstack(dot_nt(terms, g_ref[...])))
    e_copy.wait()
    from_error = unstack(dot_nt(terms, e_ref[...]))
    a_copy.wait()
    store_parts(parts_ref, unstack(dot_nn(tokens, a_ref[...])) + from_error)

    @pl.when(has_time(n_outer))
    def _():
        merged_ref[...] = dot_tn(a_ref[...], g_ref[...]) + e_ref[...].astype(F32)


def left_term(activations, out_grads, error, q_rows, n_outer):
    rank, width = q_rows.shape
    height = activations.shape[1]
    return pl.pallas_call(
        functools.partial(left_kernel, n_outer),
        name="left_term",
        out_shape=(
            pltpu.VMEM(activations.shape, BF16),
            pltpu.VMEM(out_grads.shape, BF16),
            pltpu.VMEM(error.shape, BF16),
            pltpu.VMEM(error.shape, F32),
            pltpu.VMEM((PAIR * rank, 1, height), F32),
        ),
        in_specs=[SPEC_ANY] * 4,
        out_specs=(SPEC_VMEM,) * 5,
        scratch_shapes=[pltpu.VMEM(q_rows.shape, F32), pltpu.SemaphoreType.DMA((4,))],
        compiler_params=PARAMS,
    )(in_hbm(activations), in_hbm(out_grads), in_hbm(error), in_hbm(q_rows))


def sum_kernel(in_ref, out_ref):
    total = in_ref[0]
    for at in range(1, in_ref.shape[0]):
        total = total + in_ref[at]
    for at in range(out_ref.shape[0]):
        out_ref[at] = total


def sum_parts(parts, copies):
    return pl.pallas_call(
        sum_kernel,
        name="sum_parts",
        out_shape=pltpu.VMEM((copies,) + parts.shape[1:], F32),
        in_specs=[SPEC_VMEM],
        out_specs=SPEC_VMEM,
        compiler_params=PARAMS,
    )(in_vmem(parts))


def inverse_factor(rows):
    rank = rows.shape[0]
    gram = lax.dot_general(
        rows, rows, (((1,), (1,)), ((), ())),
        precision=lax.Precision.HIGHEST, preferred_element_type=F32,
    )
    index = lax.broadcasted_iota(jnp.int32, (rank, 1), 0)
    inverse = (index == lax.broadcasted_iota(jnp.int32, (rank, rank), 1)).astype(F32)
    for step in range(rank):
        at = slice(step, step + 1)
        scale = lax.rsqrt(gram[at, at])
        column = jnp.where(index > step, gram[:, at] * scale, 0.0)
        gram = gram - column * (gram[at, :] * scale)
        row = inverse[at, :] * scale
        inverse = jnp.where(index == step, row, inverse - column * row)
    return inverse


def combine(factors, rows):
    total = factors[:, 0:1] * rows[0:1, :]
    for at in range(1, rows.shape[0]):
        total = total + factors[:, at:at + 1] * rows[at:at + 1, :]
    return total


def right_kernel(p_ref, a_ref, g_ref, e_ref, basis_ref, parts_ref):
    rank = basis_ref.shape[0]
    rows = sum_rows(p_ref, rank)
    inverse = inverse_factor(rows)
    basis_ref[...] = combine(inverse, rows)
    terms = stack(rows)
    tokens = stack(unstack(dot_nt(terms, a_ref[...])))
    products = unstack(dot_nn(tokens, g_ref[...])) + unstack(dot_nn(terms, e_ref[...]))
    store_parts(parts_ref, combine(inverse, products))


def right_term(p_parts, activations, out_grads, error, rank):
    return pl.pallas_call(
        right_kernel,
        name="right_term",
        out_shape=(
            pltpu.VMEM((rank, activations.shape[1]), F32),
            pltpu.VMEM((PAIR * rank, 1, out_grads.shape[1]), F32),
        ),
        in_specs=[SPEC_VMEM] * 4,
        out_specs=(SPEC_VMEM,) * 2,
        compiler_params=PARAMS,
    )(in_vmem(p_parts), in_vmem(activations), in_vmem(out_grads), in_vmem(error))


def error_kernel(
    n_outer, devices_all, q_ref, basis_ref, a_ref, g_ref, e_ref, merged_ref,
    error_hbm, q_hbm, basis_hbm, buf, q_buf, sems,
):
    basis_copy = pltpu.make_async_copy(basis_ref, basis_hbm, sems.at[0])
    basis_copy.start()
    rows = sum_rows(q_ref, basis_ref.shape[0])
    q_buf[...] = rows
    q_copy = pltpu.make_async_copy(q_buf, q_hbm, sems.at[1])
    q_copy.start()
    b1, b2, b3 = split(basis_ref[...] / -devices_all)
    q1, q2, q3 = split(rows)
    left = jnp.concatenate([b1, b1, b2, b1, b2, b3], axis=0)
    right = jnp.concatenate([q1, q2, q1, q3, q2, q1], axis=0)
    early = has_time(n_outer)

    @pl.when(early)
    def _():
        height = buf.shape[1]
        copies = []
        for first in range(0, height, BLOCK):
            at = slice(first, first + BLOCK)
            buf[0, at, :] = (merged_ref[at, :] + dot_tn(left[:, at], right)).astype(BF16)
            rows_at = pl.ds(first, BLOCK)
            copies.append(pltpu.make_async_copy(
                buf.at[:, rows_at], error_hbm.at[:, rows_at], sems.at[2 + first // BLOCK]
            ))
            copies[-1].start()
        for copy in copies:
            copy.wait()

    @pl.when(jnp.logical_not(early))
    def _():
        merged = dot_tn(a_ref[...], g_ref[...]) + e_ref[...].astype(F32)
        buf[0] = (merged + dot_tn(left, right)).astype(BF16)
        copy = pltpu.make_async_copy(buf, error_hbm, sems.at[2])
        copy.start()
        copy.wait()

    basis_copy.wait()
    q_copy.wait()


def new_error(q_parts, basis_rows, activations, out_grads, error, merged, n_outer, devices_all):
    height, width = error.shape
    rank = basis_rows.shape[0]
    return pl.pallas_call(
        functools.partial(error_kernel, n_outer, devices_all),
        name="new_error",
        out_shape=(
            jax.ShapeDtypeStruct((1, height, width), BF16),
            jax.ShapeDtypeStruct((rank, width), F32),
            jax.ShapeDtypeStruct((rank, height), F32),
        ),
        in_specs=[SPEC_VMEM] * 6,
        out_specs=(SPEC_ANY,) * 3,
        scratch_shapes=[
            pltpu.VMEM((1, height, width), BF16),
            pltpu.VMEM((rank, width), F32),
            pltpu.SemaphoreType.DMA((2 + height // BLOCK,)),
        ],
        compiler_params=PARAMS,
    )(*[in_vmem(x) for x in (q_parts, basis_rows, activations, out_grads, error, merged)])


def exchange(parts, axis, groups=None):
    return lax.all_to_all(parts, axis, 0, 0, axis_index_groups=groups)


def reduce_all(parts, first_pairs, last_pairs):
    rank = parts.shape[0] // PAIR
    n_outer = lax.axis_size("outer")
    within = [[x * rank + k for k in range(rank) for x in pair] for pair in first_pairs]
    across = [[x * rank + k for x in pair for k in range(rank)] for pair in last_pairs]
    parts = sum_parts(exchange(parts, "inner", within), n_outer)
    parts = sum_parts(exchange(parts, "outer"), PAIR * rank)
    return exchange(parts, "inner", across)


def local(activations, out_grads, error_in, q_init):
    n_outer = lax.axis_size("outer")
    devices_all = lax.axis_size("inner") * n_outer
    *operands, merged, parts = left_term(activations, out_grads, error_in[0], q_init.T, n_outer)
    basis_rows, parts = right_term(reduce_all(parts, FIRST, LAST), *operands, q_init.shape[1])
    error_out, q_rows, p_rows = new_error(reduce_all(parts, LAST, FIRST), basis_rows, *operands, merged, n_outer, devices_all)
    return (error_out, p_rows.T, q_rows.T)


def solution(mesh):
    placed = (
        P(("inner", "outer"), None),
        P(("inner", "outer"), None),
        P(("inner", "outer"), None, None),
        P(),
    )
    return jax.shard_map(
        local,
        mesh=mesh,
        in_specs=placed,
        out_specs=(P(("inner", "outer"), None, None), P(), P()),
        check_vma=False,
    )
```
